256 devices in a mesh: tiles: 64 (over x, z, core), rows: 4 (over y).
Axes of the slice: x: 4, y: 4, z: 8, core: 2. Of those that a mesh axis runs over, the one named last changes fastest.
Arguments:
- returns: bfloat16 [1024, 262144], P('tiles', 'rows'), may hold values from -30 to 30
- security_spans: int32 [2, 262144], P(None, 'rows'), may hold values from 0 to 1023, as said below
- band_returns: bfloat16 [1024, 1024], P('tiles', 'rows'), may hold values from -30 to 30
- band_spans: int32 [2, 1024], replicated, may hold values from 0 to 1023, as said below
- assignment: int32 [4, 128], P('rows'), may hold values from 0 to 127, as said below
Outputs:
- band_cov: bfloat16 [1024, 262144], P('tiles', 'rows')
- col_cov: bfloat16 [4, 65536, 1024], P('rows', 'tiles')
- tile_cov: bfloat16 [4, 128, 1024, 512], P('rows', 'tiles')
The draws below stay inside these ranges and needn't reach their ends.
Inputs may be any that keep to these rules, and one draw needn't show every extreme that they name: `security_spans`: first <= last for every security. `band_spans`: first <= last for every band security. `assignment`: each row is a permutation of the panels 0 to 127 of its group.
All inputs are finite; a program needn't handle non-finite values.
Results may differ from the reference program's by a relative error of at most 0.001.
Values may be sent and summed in bfloat16 or wider, within the bound.
No kernel may reach another device: no remote copies, remote signals or barrier semaphores. Data moves between devices by JAX's collectives and lax.ppermute only.
A program may use at most 128 MiB of HBM per device.

```python
import jax
import jax.numpy as jnp
from jax import lax

DAYS = 1024
PANEL = 512
BAND = 1024
PANELS_GRP = 128
SEC_GRP = 65536
NSEC = 262144
N_TILES = 64
N_ROWS = 4


def listing_spans(key, total_count, group_size, cluster):
    start_key, jitter_key, length_key = jax.random.split(key, 3)
    panel_starts = jax.random.randint(start_key, (total_count // group_size,), 0, DAYS // 2)
    firsts = jnp.repeat(panel_starts, group_size) + jax.random.randint(jitter_key, (total_count,), 0, cluster)
    lengths = jax.random.randint(length_key, (total_count,), DAYS // 8, DAYS)
    last_days = jnp.minimum(firsts + lengths, DAYS - 1)
    firsts = firsts.at[0].set(0)
    return jnp.stack([firsts, last_days]).astype(jnp.int32)


def draw_security_spans(key, part):
    shared = listing_spans(key, NSEC, PANEL, DAYS // 8)
    return shared


def draw_assignment(key, part):
    shared = listing_spans(key, NSEC, PANEL, DAYS // 8)
    spans_view = shared.reshape(2, N_ROWS, PANELS_GRP, PANEL)
    costs = jnp.max(spans_view[1], axis=2) - jnp.min(spans_view[0], axis=2)
    scores = costs * PANELS_GRP + jnp.arange(PANELS_GRP, dtype=jnp.int32)[None, :]
    ranked = jnp.argsort(scores, axis=1)
    heavy = ranked[:, ::-1][:, :N_TILES]
    light = ranked[:, :N_TILES]
    return jnp.stack([heavy, light], axis=2).reshape(N_ROWS, PANELS_GRP).astype(jnp.int32)


def draw_band_spans(key, part):
    key = jax.random.fold_in(key, 7)
    start_key, length_key = jax.random.split(key, 2)
    firsts = jax.random.randint(start_key, (BAND,), 0, 3 * DAYS // 4)
    lengths = jax.random.randint(length_key, (BAND,), DAYS // 8, DAYS)
    last_days = jnp.minimum(firsts + lengths, DAYS - 1)
    firsts = firsts.at[0].set(0)
    return jnp.stack([firsts, last_days]).astype(jnp.int32)


def draw_returns(key, part):
    key = jax.random.fold_in(key, 11)
    drift_key, noise_key = jax.random.split(key, 2)
    drift = jax.random.uniform(drift_key, (1, NSEC), minval=-1.5, maxval=1.5)
    day_scale = 4.0
    noise = jnp.clip(jax.random.normal(noise_key, (DAYS, NSEC)), -6.0, 6.0)
    return (drift + day_scale * noise).astype(jnp.bfloat16)


def draw_band_returns(key, part):
    key = jax.random.fold_in(key, 13)
    drift_key, noise_key = jax.random.split(key, 2)
    drift = jax.random.uniform(drift_key, (1, BAND), minval=-1.5, maxval=1.5)
    day_scale = 4.0
    noise = jnp.clip(jax.random.normal(noise_key, (DAYS, BAND)), -6.0, 6.0)
    return (drift + day_scale * noise).astype(jnp.bfloat16)


def setup_inputs(seed: int = 0) -> dict:
    keys = jax.random.split(jax.random.key(seed), 6)
    return {
        "returns": draw_returns(jax.random.fold_in(keys[5], 71), 0),
        "security_spans": draw_security_spans(jax.random.fold_in(keys[5], 71), 0),
        "band_returns": draw_band_returns(jax.random.fold_in(keys[5], 71), 0),
        "band_spans": draw_band_spans(jax.random.fold_in(keys[5], 71), 0),
        "assignment": draw_assignment(jax.random.fold_in(keys[5], 71), 0),
    }


def day_masks(spans_pair, day_total):
    day_index = jnp.arange(day_total, dtype=jnp.int32)[:, None]
    inside = (day_index >= spans_pair[0][None, :]) & (day_index <= spans_pair[1][None, :])
    return inside.astype(jnp.bfloat16)


def finish(product, band_width, panel_width):
    gram = product[:band_width, :panel_width]
    band_sum = product[:band_width, panel_width:]
    column_sum = product[band_width:, :panel_width]
    correlation = product[band_width:, panel_width:]
    centred = gram - band_sum * column_sum / jnp.maximum(correlation, 1.0)
    return (centred / jnp.maximum(correlation - 1.0, 1.0)).astype(jnp.bfloat16)


def pick_group(group_tiles, group_order):
    return jnp.take(group_tiles, group_order, axis=0)


def reference(returns, security_spans, band_returns, band_spans, assignment):
    band_mask = day_masks(band_spans, DAYS)
    stacked_left = jnp.concatenate([band_returns * band_mask, band_mask], axis=1)
    panel_total = NSEC // PANEL
    panel_returns = jnp.transpose(returns.reshape(DAYS, panel_total, PANEL), (1, 0, 2))
    panel_spans = jnp.transpose(security_spans.reshape(2, panel_total, PANEL), (1, 0, 2))

    def one_panel(panel_item):
        column_returns, column_spans = panel_item
        column_mask = day_masks(column_spans, DAYS)
        stacked_right = jnp.concatenate([column_returns * column_mask, column_mask], axis=1)
        product = lax.dot_general(stacked_left, stacked_right, (((0,), (0,)), ((), ())),
                                  preferred_element_type=jnp.float32)
        return finish(product, BAND, PANEL)

    tiles_all = lax.map(one_panel, (panel_returns, panel_spans))
    band_cov = jnp.transpose(tiles_all, (1, 0, 2)).reshape(BAND, NSEC)
    col_cov = jnp.transpose(band_cov).reshape(N_ROWS, SEC_GRP, BAND)
    grouped = tiles_all.reshape(N_ROWS, PANELS_GRP, BAND, PANEL)
    tile_cov = jax.vmap(pick_group)(grouped, assignment)
    return band_cov, col_cov, tile_cov
```

```python
import functools

import jax
import jax.numpy as jnp
from jax import lax
from jax.experimental import pallas as pl
from jax.experimental.pallas import tpu as pltpu
from jax.sharding import PartitionSpec as P

DAYS = 1024
PANEL = 512
BAND = 1024
VMEM_LIMIT = 40 * 1024 * 1024


def params():
    return pltpu.CompilerParams(vmem_limit_bytes=VMEM_LIMIT)


def pack_natural(returns, tile_count):
    local_days, group_width = returns.shape
    width = group_width // tile_count
    per_step = 8

    def body(in_ref, out_ref):
        for piece in range(per_step):
            out_ref[piece] = in_ref[:, piece * width : (piece + 1) * width]

    return pl.pallas_call(
        body,
        grid=(tile_count // per_step,),
        in_specs=[pl.BlockSpec((local_days, per_step * width), lambda i: (0, i))],
        out_specs=pl.BlockSpec((per_step, local_days, width), lambda i: (i, 0, 0)),
        out_shape=jax.ShapeDtypeStruct((tile_count, local_days, width), returns.dtype),
        compiler_params=params(),
        name="pack_natural",
    )(returns)


def pack_assigned(returns, order, tile_count):
    local_days, group_width = returns.shape
    panel_count = group_width // PANEL
    per_device = panel_count // tile_count
    tiles_step = tile_count // 4

    def body(order_ref, in_ref, out_ref):
        step = pl.program_id(0)
        for piece in range(tiles_step):
            for slot in range(per_device):
                panel = order_ref[(step * tiles_step + piece) * per_device + slot]
                start = pl.multiple_of(panel * PANEL, PANEL)
                out_ref[piece, :, slot * PANEL : (slot + 1) * PANEL] = in_ref[:, pl.ds(start, PANEL)]

    return pl.pallas_call(
        body,
        grid_spec=pltpu.PrefetchScalarGridSpec(
            num_scalar_prefetch=1,
            grid=(tile_count // tiles_step,),
            in_specs=[pl.BlockSpec((local_days, group_width), lambda i, order: (0, 0))],
            out_specs=pl.BlockSpec((tiles_step, local_days, per_device * PANEL), lambda i, order: (i, 0, 0)),
        ),
        out_shape=jax.ShapeDtypeStruct((tile_count, local_days, per_device * PANEL), returns.dtype),
        compiler_params=params(),
        name="pack_assigned",
    )(order, returns)


def prepare_band(band_full, band_spans):
    block = 256

    def body(spans_ref, band_ref, masked_ref, mask_ref):
        day = lax.broadcasted_iota(jnp.int32, (block, DAYS), 1)
        first = spans_ref[:, 0:1]
        last = spans_ref[:, 1:2]
        inside = (day >= first) & (day <= last)
        flipped = jnp.transpose(band_ref[...].astype(jnp.float32))
        masked_ref[...] = jnp.where(inside, flipped, 0.0).astype(jnp.bfloat16)
        mask_ref[...] = jnp.where(inside, 1.0, 0.0).astype(jnp.bfloat16)

    shape = jax.ShapeDtypeStruct((BAND, DAYS), jnp.bfloat16)
    return pl.pallas_call(
        body,
        grid=(BAND // block,),
        in_specs=[
            pl.BlockSpec((block, 2), lambda i: (i, 0)),
            pl.BlockSpec((DAYS, block), lambda i: (0, i)),
        ],
        out_specs=[pl.BlockSpec((block, DAYS), lambda i: (i, 0))] * 2,
        out_shape=[shape, shape],
        compiler_params=params(),
        name="prepare_band",
    )(jnp.transpose(band_spans), band_full)


def covariance(band_masked, band_mask, band_columns, column_spans, column_returns, width):
    first = column_spans[0:1, :]
    last = column_spans[1:2, :]
    day = lax.broadcasted_iota(jnp.int32, (DAYS, width), 0)
    inside = (day >= first) & (day <= last)
    masked = jnp.where(inside, column_returns.astype(jnp.float32), 0.0).astype(jnp.bfloat16)
    mask = jnp.where(inside, 1.0, 0.0).astype(jnp.bfloat16)
    gram = jnp.dot(band_masked, masked, preferred_element_type=jnp.float32)
    column_sum = jnp.dot(band_mask, masked, preferred_element_type=jnp.float32)
    band_sum = jnp.dot(band_masked, mask, preferred_element_type=jnp.float32)
    common = jnp.minimum(band_columns[:, 1:2], last) - jnp.maximum(band_columns[:, 0:1], first) + 1
    correlation = jnp.maximum(common, 0).astype(jnp.float32)
    at_least = jnp.maximum(correlation, 1.0)
    degrees = jnp.maximum(correlation - 1.0, 1.0)
    return (gram * at_least - band_sum * column_sum) / (at_least * degrees)


def natural_tiles(fetched, spans, band_masked, band_mask, band_columns, tile_index):
    width = 256
    total = fetched.shape[1]
    steps = total // width

    def body(where_ref, spans_ref, band_ref, masked_ref, mask_ref, in_ref, rows_ref, columns_ref):
        result = covariance(
            masked_ref[...], mask_ref[...], band_ref[...], spans_ref[...], in_ref[...], width
        )
        rows_ref[...] = result.astype(jnp.bfloat16)
        columns_ref[0] = jnp.transpose(result).astype(jnp.bfloat16)

    whole = pl.BlockSpec((BAND, DAYS), lambda i, where: (0, 0))
    return pl.pallas_call(
        body,
        grid_spec=pltpu.PrefetchScalarGridSpec(
            num_scalar_prefetch=1,
            grid=(steps,),
            in_specs=[
                pl.BlockSpec((2, width), lambda i, where: (0, where[0] * steps + i)),
                pl.BlockSpec((BAND, 2), lambda i, where: (0, 0)),
                whole,
                whole,
                pl.BlockSpec((DAYS, width), lambda i, where: (0, i)),
            ],
            out_specs=[
                pl.BlockSpec((BAND, width), lambda i, where: (0, i)),
                pl.BlockSpec((1, width, BAND), lambda i, where: (0, i, 0)),
            ],
        ),
        out_shape=[
            jax.ShapeDtypeStruct((BAND, total), jnp.bfloat16),
            jax.ShapeDtypeStruct((1, total, BAND), jnp.bfloat16),
        ],
        compiler_params=params(),
        cost_estimate=pl.CostEstimate(flops=6 * BAND * DAYS * total, bytes_accessed=12 << 20, transcendentals=0),
        name="natural_tiles",
    )(tile_index[None], spans, band_columns, band_masked, band_mask, fetched)


def assigned_tiles(fetched, spans, band_masked, band_mask, band_columns, owned):
    width = 256
    halves = PANEL // width
    slots = fetched.shape[1] // PANEL

    def body(owned_ref, spans_ref, band_ref, masked_ref, mask_ref, in_ref, out_ref):
        result = covariance(
            masked_ref[...], mask_ref[...], band_ref[...], spans_ref[...], in_ref[...], width
        )
        out_ref[0, 0] = result.astype(jnp.bfloat16)

    whole = pl.BlockSpec((BAND, DAYS), lambda i, owned: (0, 0))
    return pl.pallas_call(
        body,
        grid_spec=pltpu.PrefetchScalarGridSpec(
            num_scalar_prefetch=1,
            grid=(slots * halves,),
            in_specs=[
                pl.BlockSpec((2, width), lambda i, owned: (0, owned[i // halves] * halves + i % halves)),
                pl.BlockSpec((BAND, 2), lambda i, owned: (0, 0)),
                whole,
                whole,
                pl.BlockSpec((DAYS, width), lambda i, owned: (0, i)),
            ],
            out_specs=pl.BlockSpec((1, 1, BAND, width), lambda i, owned: (0, i // halves, 0, i % halves)),
        ),
        out_shape=jax.ShapeDtypeStruct((1, slots, BAND, PANEL), jnp.bfloat16),
        compiler_params=params(),
        cost_estimate=pl.CostEstimate(flops=6 * BAND * DAYS * slots * PANEL, bytes_accessed=10 << 20, transcendentals=0),
        name="assigned_tiles",
    )(owned, spans, band_columns, band_masked, band_mask, fetched)


def unpack_rows(arrived):
    tile_count, rows, width = arrived.shape
    per_step = 8

    def body(in_ref, out_ref):
        for piece in range(per_step):
            out_ref[:, piece * width : (piece + 1) * width] = in_ref[piece]

    return pl.pallas_call(
        body,
        grid=(tile_count // per_step,),
        in_specs=[pl.BlockSpec((per_step, rows, width), lambda i: (i, 0, 0))],
        out_specs=pl.BlockSpec((rows, per_step * width), lambda i: (0, i)),
        out_shape=jax.ShapeDtypeStruct((rows, tile_count * width), arrived.dtype),
        compiler_params=params(),
        name="unpack_rows",
    )(arrived)


def exchange(pieces):
    return lax.all_to_all(pieces, "tiles", split_axis=0, concat_axis=0, tiled=True)


def on_device(returns, security_spans, band_returns, band_spans, assignment):
    tile_count = lax.axis_size("tiles")
    tile_index = lax.axis_index("tiles")
    local_days, group_width = returns.shape
    per_device = group_width // PANEL // tile_count
    share = per_device * PANEL
    order = assignment[0]
    owned = lax.dynamic_slice_in_dim(order, tile_index * per_device, per_device)

    natural = exchange(pack_natural(returns, tile_count)).reshape(DAYS, share)
    band_part = lax.all_gather(band_returns, "rows", axis=1, tiled=True)
    band_full = lax.all_gather(band_part, "tiles", axis=0, tiled=True)
    assigned = exchange(pack_assigned(returns, order, tile_count)).reshape(DAYS, share)

    band_masked, band_mask = prepare_band(band_full, band_spans)
    band_columns = jnp.transpose(band_spans)
    rows, col_cov = natural_tiles(natural, security_spans, band_masked, band_mask, band_columns, tile_index)
    arrived = exchange(rows.reshape(tile_count, BAND // tile_count, share))
    tile_cov = assigned_tiles(assigned, security_spans, band_masked, band_mask, band_columns, owned)
    return (unpack_rows(arrived), col_cov, tile_cov)


def solution(mesh):
    placed = (P("tiles", "rows"), P(None, "rows"), P("tiles", "rows"), P(), P("rows", None))
    return jax.shard_map(
        on_device,
        mesh=mesh,
        in_specs=placed,
        out_specs=(P("tiles", "rows"), P("rows", "tiles", None), P("rows", "tiles", None, None)),
        check_vma=False,
    )
```

```python
import jax
import jax.numpy as jnp
from jax import lax
from jax.experimental import pallas as pl
from jax.experimental.pallas import tpu as pltpu
from jax.sharding import PartitionSpec as P

DAYS = 1024
PANEL = 512
BAND = 1024
N_Y = 4
N_C = 2
PART = BAND // (N_Y * N_C)
VMEM_LIMIT = 24 * 1024 * 1024


def params():
    return pltpu.CompilerParams(vmem_limit_bytes=VMEM_LIMIT)


def pack_natural(returns, band_returns, tile_count):
    local_days, group_width = returns.shape
    width = group_width // tile_count
    per_step = 16

    def body(in_ref, band_ref, out_ref):
        for piece in range(per_step):
            core = piece % N_C
            out_ref[piece, :, :width] = in_ref[:, piece * width : (piece + 1) * width]
            out_ref[piece, :, width:] = band_ref[:, core * PART : (core + 1) * PART]

    return pl.pallas_call(
        body,
        grid=(tile_count // per_step,),
        in_specs=[
            pl.BlockSpec((local_days, per_step * width), lambda i: (0, i)),
            pl.BlockSpec((local_days, N_C * PART), lambda i: (0, 0)),
        ],
        out_specs=pl.BlockSpec((per_step, local_days, width + PART), lambda i: (i, 0, 0)),
        out_shape=jax.ShapeDtypeStruct((tile_count, local_days, width + PART), returns.dtype),
        compiler_params=params(),
        name="pack_natural",
    )(returns, band_returns)


def pack_assigned(returns, order, tile_count):
    local_days, group_width = returns.shape
    panel_count = group_width // PANEL
    per_device = panel_count // tile_count
    tiles_step = tile_count // 4

    def body(order_ref, in_ref, out_ref):
        step = pl.program_id(0)
        for piece in range(tiles_step):
            for slot in range(per_device):
                panel = order_ref[(step * tiles_step + piece) * per_device + slot]
                start = pl.multiple_of(panel * PANEL, PANEL)
                out_ref[piece, :, slot * PANEL : (slot + 1) * PANEL] = in_ref[:, pl.ds(start, PANEL)]

    return pl.pallas_call(
        body,
        grid_spec=pltpu.PrefetchScalarGridSpec(
            num_scalar_prefetch=1,
            grid=(tile_count // tiles_step,),
            in_specs=[pl.BlockSpec((local_days, group_width), lambda i, order: (0, 0))],
            out_specs=pl.BlockSpec((tiles_step, local_days, per_device * PANEL), lambda i, order: (i, 0, 0)),
        ),
        out_shape=jax.ShapeDtypeStruct((tile_count, local_days, per_device * PANEL), returns.dtype),
        compiler_params=params(),
        name="pack_assigned",
    )(order, returns)


def prepare_band(own, swapped, band_columns, where):
    def body(where_ref, spans_ref, own_ref, swapped_ref, masked_ref, mask_ref):
        k = pl.program_id(0)
        y, core = where_ref[1], where_ref[2]
        day = lax.broadcasted_iota(jnp.int32, (PART, DAYS), 1)
        for side, part_ref in ((0, own_ref), (1, swapped_ref)):
            position = lax.rem(y - k + N_Y, N_Y) * N_C + lax.rem(core + side, N_C)
            rows = pl.ds(pl.multiple_of(position * PART, PART), PART)
            inside = (day >= spans_ref[rows, 0:1]) & (day <= spans_ref[rows, 1:2])
            flipped = jnp.transpose(part_ref[0].astype(jnp.float32))
            masked_ref[rows, :] = jnp.where(inside, flipped, 0.0).astype(jnp.bfloat16)
            mask_ref[rows, :] = jnp.where(inside, 1.0, 0.0).astype(jnp.bfloat16)

    part = pl.BlockSpec((1, DAYS, PART), lambda i, where: (i, 0, 0))
    shape = jax.ShapeDtypeStruct((BAND, DAYS), jnp.bfloat16)
    return pl.pallas_call(
        body,
        grid_spec=pltpu.PrefetchScalarGridSpec(
            num_scalar_prefetch=1,
            grid=(N_Y,),
            in_specs=[pl.BlockSpec((BAND, 2), lambda i, where: (0, 0)), part, part],
            out_specs=[pl.BlockSpec((BAND, DAYS), lambda i, where: (0, 0))] * 2,
        ),
        out_shape=[shape, shape],
        compiler_params=params(),
        name="prepare_band",
    )(where, band_columns, own, swapped)


def covariance(band_masked, band_mask, band_columns, column_spans, column_returns, width):
    first = column_spans[0:1, :]
    last = column_spans[1:2, :]
    day = lax.broadcasted_iota(jnp.int32, (DAYS, width), 0)
    inside = (day >= first) & (day <= last)
    masked = jnp.where(inside, column_returns.astype(jnp.float32), 0.0).astype(jnp.bfloat16)
    mask = jnp.where(inside, 1.0, 0.0).astype(jnp.bfloat16)
    gram = jnp.dot(band_masked, masked, preferred_element_type=jnp.float32)
    column_sum = jnp.dot(band_mask, masked, preferred_element_type=jnp.float32)
    band_sum = jnp.dot(band_masked, mask, preferred_element_type=jnp.float32)
    common = jnp.minimum(band_columns[:, 1:2], last) - jnp.maximum(band_columns[:, 0:1], first) + 1
    correlation = jnp.maximum(common, 0).astype(jnp.float32)
    at_least = jnp.maximum(correlation, 1.0)
    degrees = jnp.maximum(correlation - 1.0, 1.0)
    return (gram * at_least - band_sum * column_sum) / (at_least * degrees)


def natural_tiles(fetched, spans, band_masked, band_mask, band_columns, where, total):
    width = 256
    steps = total // width

    def body(where_ref, spans_ref, band_ref, masked_ref, mask_ref, in_ref, rows_ref, columns_ref):
        result = covariance(
            masked_ref[...], mask_ref[...], band_ref[...], spans_ref[...], in_ref[...], width
        )
        rows_ref[...] = result.astype(jnp.bfloat16)
        columns_ref[0] = jnp.transpose(result).astype(jnp.bfloat16)

    whole = pl.BlockSpec((BAND, DAYS), lambda i, where: (0, 0))
    return pl.pallas_call(
        body,
        grid_spec=pltpu.PrefetchScalarGridSpec(
            num_scalar_prefetch=1,
            grid=(steps,),
            in_specs=[
                pl.BlockSpec((2, width), lambda i, where: (0, where[0] * steps + i)),
                pl.BlockSpec((BAND, 2), lambda i, where: (0, 0)),
                whole,
                whole,
                pl.BlockSpec((DAYS, width), lambda i, where: (0, i)),
            ],
            out_specs=[
                pl.BlockSpec((BAND, width), lambda i, where: (0, i)),
                pl.BlockSpec((1, width, BAND), lambda i, where: (0, i, 0)),
            ],
        ),
        out_shape=[
            jax.ShapeDtypeStruct((BAND, total), jnp.bfloat16),
            jax.ShapeDtypeStruct((1, total, BAND), jnp.bfloat16),
        ],
        compiler_params=params(),
        cost_estimate=pl.CostEstimate(flops=6 * BAND * DAYS * total, bytes_accessed=12 << 20, transcendentals=0),
        name="natural_tiles",
    )(where, spans, band_columns, band_masked, band_mask, fetched)


def assigned_tiles(fetched, spans, band_masked, band_mask, band_columns, owned):
    width = 256
    halves = PANEL // width
    slots = fetched.shape[1] // PANEL

    def body(owned_ref, spans_ref, band_ref, masked_ref, mask_ref, in_ref, out_ref):
        result = covariance(
            masked_ref[...], mask_ref[...], band_ref[...], spans_ref[...], in_ref[...], width
        )
        out_ref[0, 0] = result.astype(jnp.bfloat16)

    whole = pl.BlockSpec((BAND, DAYS), lambda i, owned: (0, 0))
    return pl.pallas_call(
        body,
        grid_spec=pltpu.PrefetchScalarGridSpec(
            num_scalar_prefetch=1,
            grid=(slots * halves,),
            in_specs=[
                pl.BlockSpec((2, width), lambda i, owned: (0, owned[i // halves] * halves + i % halves)),
                pl.BlockSpec((BAND, 2), lambda i, owned: (0, 0)),
                whole,
                whole,
                pl.BlockSpec((DAYS, width), lambda i, owned: (0, i)),
            ],
            out_specs=pl.BlockSpec((1, 1, BAND, width), lambda i, owned: (0, i // halves, 0, i % halves)),
        ),
        out_shape=jax.ShapeDtypeStruct((1, slots, BAND, PANEL), jnp.bfloat16),
        compiler_params=params(),
        cost_estimate=pl.CostEstimate(flops=6 * BAND * DAYS * slots * PANEL, bytes_accessed=10 << 20, transcendentals=0),
        name="assigned_tiles",
    )(owned, spans, band_columns, band_masked, band_mask, fetched)


def unpack_rows(arrived):
    tile_count, rows, width = arrived.shape
    per_step = 8

    def body(in_ref, out_ref):
        for piece in range(per_step):
            out_ref[:, piece * width : (piece + 1) * width] = in_ref[piece]

    return pl.pallas_call(
        body,
        grid=(tile_count // per_step,),
        in_specs=[pl.BlockSpec((per_step, rows, width), lambda i: (i, 0, 0))],
        out_specs=pl.BlockSpec((rows, per_step * width), lambda i: (0, i)),
        out_shape=jax.ShapeDtypeStruct((rows, tile_count * width), arrived.dtype),
        compiler_params=params(),
        name="unpack_rows",
    )(arrived)


def exchange(pieces):
    return lax.all_to_all(pieces, "tiles", split_axis=0, concat_axis=0, tiled=True)


def shift_rows(array, step):
    return lax.ppermute(array, "rows", [(y, (y + step) % N_Y) for y in range(N_Y)])


def swap_cores(array):
    return lax.ppermute(array, "tiles", [(i, i ^ 1) for i in range(lax.axis_size("tiles"))])


def on_device(returns, security_spans, band_returns, band_spans, assignment):
    tile_count = lax.axis_size("tiles")
    tile_index = lax.axis_index("tiles")
    local_days, group_width = returns.shape
    per_device = group_width // PANEL // tile_count
    share = per_device * PANEL
    order = assignment[0]
    owned = lax.dynamic_slice_in_dim(order, tile_index * per_device, per_device)

    where = jnp.stack([tile_index, lax.axis_index("rows"), tile_index % N_C]).astype(jnp.int32)

    natural = exchange(pack_natural(returns, band_returns, tile_count)).reshape(DAYS, share + PART)
    assigned = exchange(pack_assigned(returns, order, tile_count)).reshape(DAYS, share)

    mine = natural[:, share:]
    own = jnp.stack([mine] + [shift_rows(mine, k) for k in range(1, N_Y)])
    swapped = swap_cores(own)
    band_columns = jnp.transpose(band_spans)
    band_masked, band_mask = prepare_band(own, swapped, band_columns, where)
    rows, col_cov = natural_tiles(natural, security_spans, band_masked, band_mask, band_columns, where, share)
    arrived = exchange(rows.reshape(tile_count, BAND // tile_count, share))
    tile_cov = assigned_tiles(assigned, security_spans, band_masked, band_mask, band_columns, owned)
    return (unpack_rows(arrived), col_cov, tile_cov)


def solution(mesh):
    placed = (P("tiles", "rows"), P(None, "rows"), P("tiles", "rows"), P(), P("rows", None))
    return jax.shard_map(
        on_device,
        mesh=mesh,
        in_specs=placed,
        out_specs=(P("tiles", "rows"), P("rows", "tiles", None), P("rows", "tiles", None, None)),
        check_vma=False,
    )
```

```python
import jax
import jax.numpy as jnp
from jax import lax
from jax.experimental import pallas as pl
from jax.experimental.pallas import tpu as pltpu
from jax.sharding import PartitionSpec as P

DAYS = 1024
PANEL = 512
BAND = 1024
N_Y = 4
N_C = 2
PART = BAND // (N_Y * N_C)
VMEM_LIMIT = 24 * 1024 * 1024
LARGE = 56 * 1024 * 1024


def params(limit=VMEM_LIMIT):
    return pltpu.CompilerParams(vmem_limit_bytes=limit)


def pack_natural(returns, band_returns, tile_count):
    local_days, group_width = returns.shape
    width = group_width // tile_count
    per_step = 32

    def body(in_ref, band_ref, out_ref):
        for piece in range(per_step):
            core = piece % N_C
            out_ref[piece, :, :width] = in_ref[:, piece * width : (piece + 1) * width]
            out_ref[piece, :, width:] = band_ref[:, core * PART : (core + 1) * PART]

    return pl.pallas_call(
        body,
        grid=(tile_count // per_step,),
        in_specs=[
            pl.BlockSpec((local_days, per_step * width), lambda i: (0, i)),
            pl.BlockSpec((local_days, N_C * PART), lambda i: (0, 0)),
        ],
        out_specs=pl.BlockSpec((per_step, local_days, width + PART), lambda i: (i, 0, 0)),
        out_shape=jax.ShapeDtypeStruct((tile_count, local_days, width + PART), returns.dtype),
        compiler_params=params(LARGE),
        name="pack_natural",
    )(returns, band_returns)


def pack_assigned(returns, order, tile_count):
    local_days, group_width = returns.shape
    panel_count = group_width // PANEL
    per_device = panel_count // tile_count
    tiles_step = tile_count // 4

    def body(order_ref, in_ref, out_ref):
        step = pl.program_id(0)
        for piece in range(tiles_step):
            for slot in range(per_device):
                panel = order_ref[(step * tiles_step + piece) * per_device + slot]
                start = pl.multiple_of(panel * PANEL, PANEL)
                out_ref[piece, :, slot * PANEL : (slot + 1) * PANEL] = in_ref[:, pl.ds(start, PANEL)]

    return pl.pallas_call(
        body,
        grid_spec=pltpu.PrefetchScalarGridSpec(
            num_scalar_prefetch=1,
            grid=(tile_count // tiles_step,),
            in_specs=[pl.BlockSpec((local_days, group_width), lambda i, order: (0, 0))],
            out_specs=pl.BlockSpec((tiles_step, local_days, per_device * PANEL), lambda i, order: (i, 0, 0)),
        ),
        out_shape=jax.ShapeDtypeStruct((tile_count, local_days, per_device * PANEL), returns.dtype),
        compiler_params=params(),
        name="pack_assigned",
    )(order, returns)


def prepare_band(own, swapped, band_columns, where):
    def body(where_ref, spans_ref, own_ref, swapped_ref, masked_ref, mask_ref):
        k = pl.program_id(0)
        y, core = where_ref[1], where_ref[2]
        day = lax.broadcasted_iota(jnp.int32, (PART, DAYS), 1)
        for side, part_ref in ((0, own_ref), (1, swapped_ref)):
            position = lax.rem(y - k + N_Y, N_Y) * N_C + lax.rem(core + side, N_C)
            rows = pl.ds(pl.multiple_of(position * PART, PART), PART)
            inside = (day >= spans_ref[rows, 0:1]) & (day <= spans_ref[rows, 1:2])
            flipped = jnp.transpose(part_ref[0].astype(jnp.float32))
            masked_ref[rows, :] = jnp.where(inside, flipped, 0.0).astype(jnp.bfloat16)
            mask_ref[rows, :] = jnp.where(inside, 1.0, 0.0).astype(jnp.bfloat16)

    part = pl.BlockSpec((1, DAYS, PART), lambda i, where: (i, 0, 0))
    shape = jax.ShapeDtypeStruct((BAND, DAYS), jnp.bfloat16)
    return pl.pallas_call(
        body,
        grid_spec=pltpu.PrefetchScalarGridSpec(
            num_scalar_prefetch=1,
            grid=(N_Y,),
            in_specs=[pl.BlockSpec((BAND, 2), lambda i, where: (0, 0)), part, part],
            out_specs=[pl.BlockSpec((BAND, DAYS), lambda i, where: (0, 0))] * 2,
        ),
        out_shape=[shape, shape],
        compiler_params=params(),
        name="prepare_band",
    )(where, band_columns, own, swapped)


def covariance(band_masked, band_mask, band_columns, column_spans, column_returns, width):
    first = column_spans[0:1, :]
    last = column_spans[1:2, :]
    day = lax.broadcasted_iota(jnp.int32, (DAYS, width), 0)
    inside = (day >= first) & (day <= last)
    masked = jnp.where(inside, column_returns.astype(jnp.float32), 0.0).astype(jnp.bfloat16)
    mask = jnp.where(inside, 1.0, 0.0).astype(jnp.bfloat16)
    gram = jnp.dot(band_masked, masked, preferred_element_type=jnp.float32)
    column_sum = jnp.dot(band_mask, masked, preferred_element_type=jnp.float32)
    band_sum = jnp.dot(band_masked, mask, preferred_element_type=jnp.float32)
    common = jnp.minimum(band_columns[:, 1:2], last) - jnp.maximum(band_columns[:, 0:1], first) + 1
    correlation = jnp.maximum(common, 0).astype(jnp.float32)
    at_least = jnp.maximum(correlation, 1.0)
    degrees = jnp.maximum(correlation - 1.0, 1.0)
    return (gram * at_least - band_sum * column_sum) / (at_least * degrees)


def natural_tiles(fetched, spans, band_masked, band_mask, band_columns, where, total):
    width = 256
    steps = total // width

    def body(where_ref, spans_ref, band_ref, masked_ref, mask_ref, in_ref, rows_ref, columns_ref):
        result = covariance(
            masked_ref[...], mask_ref[...], band_ref[...], spans_ref[...], in_ref[...], width
        )
        rows_ref[...] = result.astype(jnp.bfloat16)
        columns_ref[0] = jnp.transpose(result).astype(jnp.bfloat16)

    whole = pl.BlockSpec((BAND, DAYS), lambda i, where: (0, 0))
    return pl.pallas_call(
        body,
        grid_spec=pltpu.PrefetchScalarGridSpec(
            num_scalar_prefetch=1,
            grid=(steps,),
            in_specs=[
                pl.BlockSpec((2, width), lambda i, where: (0, where[0] * steps + i)),
                pl.BlockSpec((BAND, 2), lambda i, where: (0, 0)),
                whole,
                whole,
                pl.BlockSpec((DAYS, width), lambda i, where: (0, i)),
            ],
            out_specs=[
                pl.BlockSpec((BAND, width), lambda i, where: (0, i)),
                pl.BlockSpec((1, width, BAND), lambda i, where: (0, i, 0)),
            ],
        ),
        out_shape=[
            jax.ShapeDtypeStruct((BAND, total), jnp.bfloat16),
            jax.ShapeDtypeStruct((1, total, BAND), jnp.bfloat16),
        ],
        compiler_params=params(),
        cost_estimate=pl.CostEstimate(flops=6 * BAND * DAYS * total, bytes_accessed=12 << 20, transcendentals=0),
        name="natural_tiles",
    )(where, spans, band_columns, band_masked, band_mask, fetched)


def assigned_tiles(fetched, spans, band_masked, band_mask, band_columns, owned):
    width = 256
    halves = PANEL // width
    slots = fetched.shape[1] // PANEL

    def body(owned_ref, spans_ref, band_ref, masked_ref, mask_ref, in_ref, out_ref):
        result = covariance(
            masked_ref[...], mask_ref[...], band_ref[...], spans_ref[...], in_ref[...], width
        )
        out_ref[0, 0] = result.astype(jnp.bfloat16)

    whole = pl.BlockSpec((BAND, DAYS), lambda i, owned: (0, 0))
    return pl.pallas_call(
        body,
        grid_spec=pltpu.PrefetchScalarGridSpec(
            num_scalar_prefetch=1,
            grid=(slots * halves,),
            in_specs=[
                pl.BlockSpec((2, width), lambda i, owned: (0, owned[i // halves] * halves + i % halves)),
                pl.BlockSpec((BAND, 2), lambda i, owned: (0, 0)),
                whole,
                whole,
                pl.BlockSpec((DAYS, width), lambda i, owned: (0, i)),
            ],
            out_specs=pl.BlockSpec((1, 1, BAND, width), lambda i, owned: (0, i // halves, 0, i % halves)),
        ),
        out_shape=jax.ShapeDtypeStruct((1, slots, BAND, PANEL), jnp.bfloat16),
        compiler_params=params(),
        cost_estimate=pl.CostEstimate(flops=6 * BAND * DAYS * slots * PANEL, bytes_accessed=10 << 20, transcendentals=0),
        name="assigned_tiles",
    )(owned, spans, band_columns, band_masked, band_mask, fetched)


def unpack_rows(arrived):
    tile_count, rows, width = arrived.shape
    per_step = 32

    def body(in_ref, out_ref):
        for piece in range(per_step):
            out_ref[:, piece * width : (piece + 1) * width] = in_ref[piece]

    return pl.pallas_call(
        body,
        grid=(tile_count // per_step,),
        in_specs=[pl.BlockSpec((per_step, rows, width), lambda i: (i, 0, 0))],
        out_specs=pl.BlockSpec((rows, per_step * width), lambda i: (0, i)),
        out_shape=jax.ShapeDtypeStruct((rows, tile_count * width), arrived.dtype),
        compiler_params=params(),
        name="unpack_rows",
    )(arrived)


def exchange(pieces):
    return lax.all_to_all(pieces, "tiles", split_axis=0, concat_axis=0, tiled=True)


def shift_rows(array, step):
    return lax.ppermute(array, "rows", [(y, (y + step) % N_Y) for y in range(N_Y)])


def swap_cores(array):
    return lax.ppermute(array, "tiles", [(i, i ^ 1) for i in range(lax.axis_size("tiles"))])


def on_device(returns, security_spans, band_returns, band_spans, assignment):
    tile_count = lax.axis_size("tiles")
    tile_index = lax.axis_index("tiles")
    local_days, group_width = returns.shape
    per_device = group_width // PANEL // tile_count
    share = per_device * PANEL
    order = assignment[0]
    owned = lax.dynamic_slice_in_dim(order, tile_index * per_device, per_device)

    where = jnp.stack([tile_index, lax.axis_index("rows"), tile_index % N_C]).astype(jnp.int32)

    natural = exchange(pack_natural(returns, band_returns, tile_count)).reshape(DAYS, share + PART)
    assigned = exchange(pack_assigned(returns, order, tile_count)).reshape(DAYS, share)

    mine = natural[:, share:]
    own = jnp.stack([mine] + [shift_rows(mine, k) for k in range(1, N_Y)])
    swapped = swap_cores(own)
    band_columns = jnp.transpose(band_spans)
    band_masked, band_mask = prepare_band(own, swapped, band_columns, where)
    rows, col_cov = natural_tiles(natural, security_spans, band_masked, band_mask, band_columns, where, share)
    arrived = exchange(rows.reshape(tile_count, BAND // tile_count, share))
    tile_cov = assigned_tiles(assigned, security_spans, band_masked, band_mask, band_columns, owned)
    return (unpack_rows(arrived), col_cov, tile_cov)


def solution(mesh):
    placed = (P("tiles", "rows"), P(None, "rows"), P("tiles", "rows"), P(), P("rows", None))
    return jax.shard_map(
        on_device,
        mesh=mesh,
        in_specs=placed,
        out_specs=(P("tiles", "rows"), P("rows", "tiles", None), P("rows", "tiles", None, None)),
        check_vma=False,
    )
```

```python
import jax
import jax.numpy as jnp
from jax import lax
from jax.experimental import pallas as pl
from jax.experimental.pallas import tpu as pltpu
from jax.sharding import PartitionSpec as P

DAYS = 1024
PANEL = 512
BAND = 1024
N_X, N_Z, N_C, N_Y = 4, 8, 2, 4
PLANE = N_X * N_Z * N_C
LOCAL = DAYS // PLANE
QUARTER = BAND // N_Y
SLOTS = 2
SHARE = SLOTS * PANEL
WIDTH = 256
MAIN = SHARE + PANEL
FORCED = (1, 7, 2, 6, 3, 5, 4)
PLANE_X = N_X * N_C
SHIFTS = [(0, 0), (1, 0), (3, 0), (2, 0), (0, 1), (1, 1), (3, 1), (2, 1)]
VMEM_LIMIT = 56 * 1024 * 1024


def params(limit=VMEM_LIMIT):
    return pltpu.CompilerParams(vmem_limit_bytes=limit)


def shape(*sizes, dtype=jnp.bfloat16):
    return jax.ShapeDtypeStruct(sizes, dtype)


def whole(*sizes):
    return pl.BlockSpec(sizes, lambda i, *_: (0,) * len(sizes))


def pack(returns, order, where):
    def body(order_ref, where_ref, in_ref, main_ref, *out_refs):
        def panel(owner, slot):
            start = pl.multiple_of(order_ref[owner * SLOTS + slot] * PANEL, PANEL)
            return in_ref[:, pl.ds(start, PANEL)]

        for k in range(N_Z):
            z = lax.rem(where_ref[1] + k, N_Z)
            for x in range(N_X):
                for core in range(N_C):
                    owner = (x * N_Z + z) * N_C + core
                    place = x * N_C + core
                    out_refs[k][:, place * PANEL : (place + 1) * PANEL] = panel(owner, 1)
        for owner in range(PLANE):
            main_ref[owner, :, :SHARE] = in_ref[:, owner * SHARE : (owner + 1) * SHARE]
            main_ref[owner, :, SHARE:] = panel(owner, 0)

    return pl.pallas_call(
        body,
        grid_spec=pltpu.PrefetchScalarGridSpec(
            num_scalar_prefetch=2,
            grid=(1,),
            in_specs=[whole(*returns.shape)],
            out_specs=[whole(PLANE, LOCAL, MAIN)] + [whole(LOCAL, PLANE_X * PANEL)] * N_Z,
        ),
        out_shape=[shape(PLANE, LOCAL, MAIN)] + [shape(LOCAL, PLANE_X * PANEL)] * N_Z,
        compiler_params=params(),
        name="pack",
    )(order, where, returns)


def repack(pieces, where):
    def body(where_ref, *refs):
        x, z, core = where_ref[0], where_ref[1], where_ref[2]
        for k in range(N_Z):
            rows = pl.ds(pl.multiple_of(lax.rem(z - k + N_Z, N_Z) * LOCAL, LOCAL), LOCAL)
            for j, (dx, dc) in enumerate(SHIFTS):
                target = lax.rem(x + dx, N_X) * N_C + lax.rem(core + dc, N_C)
                start = pl.multiple_of(target * PANEL, PANEL)
                refs[N_Z + j][rows, :] = refs[k][:, pl.ds(start, PANEL)]

    return pl.pallas_call(
        body,
        grid_spec=pltpu.PrefetchScalarGridSpec(
            num_scalar_prefetch=1,
            grid=(1,),
            in_specs=[whole(LOCAL, PLANE_X * PANEL)] * N_Z,
            out_specs=[whole(N_Z * LOCAL, PANEL)] * len(SHIFTS),
        ),
        out_shape=[shape(N_Z * LOCAL, PANEL)] * len(SHIFTS),
        compiler_params=params(),
        name="repack",
    )(where, *pieces)


def prepare_band(own, swapped, band_columns, where):
    def body(where_ref, spans_ref, own_ref, swapped_ref, masked_ref, mask_ref, days):
        k = pl.program_id(0)
        x, z, core, y = where_ref[0], where_ref[1], where_ref[2], where_ref[3]
        for side, part_ref in ((0, own_ref), (1, swapped_ref)):
            for j in range(N_X):
                for m in range(N_Z):
                    source = lax.rem(x - j + N_X, N_X) * N_Z + lax.rem(z - m // 2 - 4 * (m % 2) + N_Z, N_Z)
                    source = source * N_C + lax.rem(core + side, N_C)
                    days[pl.ds(pl.multiple_of(source * LOCAL, LOCAL), LOCAL), :] = part_ref[0, j, m * LOCAL : (m + 1) * LOCAL]
        rows = pl.ds(pl.multiple_of(lax.rem(y - k + N_Y, N_Y) * QUARTER, QUARTER), QUARTER)
        day = lax.broadcasted_iota(jnp.int32, (QUARTER, DAYS), 1)
        inside = (day >= spans_ref[rows, 0:1]) & (day <= spans_ref[rows, 1:2])
        flipped = jnp.transpose(days[...].astype(jnp.float32))
        masked_ref[rows, :] = jnp.where(inside, flipped, 0.0).astype(jnp.bfloat16)
        mask_ref[rows, :] = jnp.where(inside, 1.0, 0.0).astype(jnp.bfloat16)

    part = pl.BlockSpec((1, N_X, N_Z * LOCAL, QUARTER), lambda i, where: (i, 0, 0, 0))
    return pl.pallas_call(
        body,
        grid_spec=pltpu.PrefetchScalarGridSpec(
            num_scalar_prefetch=1,
            grid=(N_Y,),
            in_specs=[whole(BAND, 2), part, part],
            out_specs=[whole(BAND, DAYS)] * 2,
            scratch_shapes=[pltpu.VMEM((DAYS, QUARTER), jnp.bfloat16)],
        ),
        out_shape=[shape(BAND, DAYS)] * 2,
        compiler_params=params(),
        name="prepare_band",
    )(where, band_columns, own, swapped)


def listed(spans):
    day = lax.broadcasted_iota(jnp.int32, (DAYS, WIDTH), 0)
    return (day >= spans[0:1, :]) & (day <= spans[1:2, :])


def masked_returns(inside, column_returns):
    return jnp.where(inside, column_returns.astype(jnp.float32), 0.0).astype(jnp.bfloat16)


def factors(inside, spans, band_masked, band_columns):
    mask = jnp.where(inside, 1.0, 0.0).astype(jnp.bfloat16)
    band_sum = jnp.dot(band_masked, mask, preferred_element_type=jnp.float32)
    common = jnp.minimum(band_columns[:, 1:2], spans[1:2, :]) - jnp.maximum(band_columns[:, 0:1], spans[0:1, :]) + 1
    correlation = jnp.maximum(common, 0).astype(jnp.float32)
    scale = 1.0 / jnp.maximum(correlation - 1.0, 1.0)
    return scale, band_sum * scale / jnp.maximum(correlation, 1.0)


def covariance(spans, band_columns, band_masked, band_mask, column_returns):
    inside = listed(spans)
    masked = masked_returns(inside, column_returns)
    scale, mean = factors(inside, spans, band_masked, band_columns)
    gram = jnp.dot(band_masked, masked, preferred_element_type=jnp.float32)
    column_sum = jnp.dot(band_mask, masked, preferred_element_type=jnp.float32)
    return (gram * scale - column_sum * mean).astype(jnp.bfloat16)


def natural_rows(fetched, spans, band_masked, band_mask, band_columns, where):
    steps = SHARE // WIDTH

    def body(where_ref, spans_ref, band_ref, masked_ref, mask_ref, in_ref, rows_ref):
        rows_ref[...] = covariance(
            spans_ref[...], band_ref[...], masked_ref[...], mask_ref[...], in_ref[...]
        )

    return pl.pallas_call(
        body,
        grid_spec=pltpu.PrefetchScalarGridSpec(
            num_scalar_prefetch=1,
            grid=(steps,),
            in_specs=[
                pl.BlockSpec((2, WIDTH), lambda i, where: (0, where[4] * steps + i)),
                whole(BAND, 2),
                whole(BAND, DAYS),
                whole(BAND, DAYS),
                pl.BlockSpec((DAYS, WIDTH), lambda i, where: (0, i)),
            ],
            out_specs=pl.BlockSpec((BAND, WIDTH), lambda i, where: (0, i)),
        ),
        out_shape=shape(BAND, SHARE),
        compiler_params=params(),
        cost_estimate=pl.CostEstimate(flops=6 * BAND * DAYS * SHARE, bytes_accessed=12 << 20, transcendentals=0),
        name="natural_rows",
    )(where, spans, band_columns, band_masked, band_mask, fetched)


def flip(rows):
    def body(in_ref, out_ref):
        out_ref[0] = jnp.transpose(in_ref[...].astype(jnp.float32)).astype(jnp.bfloat16)

    return pl.pallas_call(
        body,
        grid=(SHARE // WIDTH,),
        in_specs=[pl.BlockSpec((BAND, WIDTH), lambda i: (0, i))],
        out_specs=pl.BlockSpec((1, WIDTH, BAND), lambda i: (0, i, 0)),
        out_shape=shape(1, SHARE, BAND),
        compiler_params=params(),
        name="flip",
    )(rows)


def assigned_first(fetched, spans, band_masked, band_mask, band_columns, owned):
    halves = PANEL // WIDTH

    def body(owned_ref, spans_ref, band_ref, masked_ref, mask_ref, in_ref, out_ref):
        out_ref[0, 0] = covariance(
            spans_ref[...], band_ref[...], masked_ref[...], mask_ref[...], in_ref[...]
        )

    return pl.pallas_call(
        body,
        grid_spec=pltpu.PrefetchScalarGridSpec(
            num_scalar_prefetch=1,
            grid=(halves,),
            in_specs=[
                pl.BlockSpec((2, WIDTH), lambda i, owned: (0, owned[0] * halves + i)),
                whole(BAND, 2),
                whole(BAND, DAYS),
                whole(BAND, DAYS),
                pl.BlockSpec((DAYS, WIDTH), lambda i, owned: (0, SHARE // WIDTH + i)),
            ],
            out_specs=pl.BlockSpec((1, 1, BAND, WIDTH), lambda i, owned: (0, 0, 0, i)),
        ),
        out_shape=shape(1, SLOTS, BAND, PANEL),
        compiler_params=params(),
        cost_estimate=pl.CostEstimate(flops=6 * BAND * DAYS * PANEL, bytes_accessed=6 << 20, transcendentals=0),
        name="assigned_first",
    )(owned, spans, band_columns, band_masked, band_mask, fetched)


def assigned_second(tiles, chunks, spans, band_masked, band_mask, band_columns, owned, where):
    halves = PANEL // WIDTH

    def body(owned_ref, where_ref, tiles_ref, spans_ref, band_ref, masked_ref, mask_ref, *refs):
        out_ref, days = refs[-2:]
        for j, (dx, dc) in enumerate(SHIFTS):
            x = lax.rem(where_ref[0] - dx + N_X, N_X)
            core = lax.rem(where_ref[2] + dc, N_C)
            for z in range(N_Z):
                start = pl.multiple_of(((x * N_Z + z) * N_C + core) * LOCAL, LOCAL)
                days[pl.ds(start, LOCAL), :] = refs[j][z * LOCAL : (z + 1) * LOCAL, :]
        out_ref[0, 0] = covariance(
            spans_ref[...], band_ref[...], masked_ref[...], mask_ref[...], days[...]
        )

    return pl.pallas_call(
        body,
        grid_spec=pltpu.PrefetchScalarGridSpec(
            num_scalar_prefetch=2,
            grid=(halves,),
            in_specs=[
                pl.BlockSpec(memory_space=pl.ANY),
                pl.BlockSpec((2, WIDTH), lambda i, owned, where: (0, owned[1] * halves + i)),
                whole(BAND, 2),
                whole(BAND, DAYS),
                whole(BAND, DAYS),
            ]
            + [pl.BlockSpec((N_Z * LOCAL, WIDTH), lambda i, owned, where: (0, i))] * len(SHIFTS),
            out_specs=pl.BlockSpec((1, 1, BAND, WIDTH), lambda i, owned, where: (0, 1, 0, i)),
            scratch_shapes=[pltpu.VMEM((DAYS, WIDTH), jnp.bfloat16)],
        ),
        out_shape=shape(1, SLOTS, BAND, PANEL),
        input_output_aliases={2: 0},
        compiler_params=params(),
        cost_estimate=pl.CostEstimate(flops=6 * BAND * DAYS * PANEL, bytes_accessed=6 << 20, transcendentals=0),
        name="assigned_second",
    )(owned, where, tiles, spans, band_columns, band_masked, band_mask, *chunks)


def unpack_rows(arrived):
    per_step = 32

    def body(in_ref, out_ref):
        for piece in range(per_step):
            out_ref[:, piece * SHARE : (piece + 1) * SHARE] = in_ref[piece]

    return pl.pallas_call(
        body,
        grid=(PLANE // per_step,),
        in_specs=[pl.BlockSpec((per_step, LOCAL, SHARE), lambda i: (i, 0, 0))],
        out_specs=pl.BlockSpec((LOCAL, per_step * SHARE), lambda i: (0, i)),
        out_shape=shape(LOCAL, PLANE * SHARE),
        compiler_params=params(24 * 1024 * 1024),
        name="unpack_rows",
    )(arrived)


def exchange(pieces):
    return lax.all_to_all(pieces, "tiles", split_axis=0, concat_axis=0, tiled=True)


def shift_rows(array, step):
    return lax.ppermute(array, "rows", [(y, (y + step) % N_Y) for y in range(N_Y)])


def swap(array, bit):
    return lax.ppermute(array, "tiles", [(i, i ^ bit) for i in range(PLANE)])


def shift(array, dx, dz, dc):
    def to(i):
        x, z, core = i // (N_Z * N_C) + dx, i // N_C % N_Z + dz, i % N_C + dc
        return (x % N_X * N_Z + z % N_Z) * N_C + core % N_C

    return lax.ppermute(array, "tiles", [(i, to(i)) for i in range(PLANE)])


def on_device(returns, security_spans, band_returns, band_spans, assignment):
    tile_index = lax.axis_index("tiles")
    x, z, core = tile_index // (N_Z * N_C), (tile_index // N_C) % N_Z, tile_index % N_C
    where = jnp.stack([x, z, core, lax.axis_index("rows"), tile_index]).astype(jnp.int32)
    order = assignment[0]
    owned = lax.dynamic_slice_in_dim(order, tile_index * SLOTS, SLOTS)
    band_columns = jnp.transpose(band_spans)

    packed, *sends = pack(returns, order, where)
    pair = jnp.concatenate([band_returns, shift(band_returns, 0, 4, 0)])
    pair, packed, sends = lax.optimization_barrier((pair, packed, sends))
    share = jnp.concatenate([pair] + [shift(pair, 0, k, 0) for k in range(1, 4)])
    packed, share = lax.optimization_barrier((packed, share))
    fetched = exchange(packed).reshape(DAYS, MAIN)
    own = jnp.stack([share] + [shift(share, j, 0, 0) for j in range(1, N_X)])
    own = jnp.stack([own] + [shift_rows(own, k) for k in range(1, N_Y)])
    swapped = swap(own, 1)
    band = prepare_band(own, swapped, band_columns, where)
    *band, sends = lax.optimization_barrier((*band, sends))
    pieces = [sends[0]] + [shift(sends[k], 0, k, 0) for k in range(1, N_Z)]

    rows = natural_rows(fetched, security_spans, *band, band_columns, where)
    rows, fetched, *forced = lax.optimization_barrier((rows, fetched, *(pieces[k] for k in FORCED)))
    for k, piece in zip(FORCED, forced):
        pieces[k] = piece
    arrived = exchange(rows.reshape(PLANE, BAND // PLANE, SHARE))
    col_cov = flip(rows)
    tiles = assigned_first(fetched, security_spans, *band, band_columns, owned)
    chunks = [shift(part, dx, 0, dc) if dx or dc else part for part, (dx, dc) in zip(repack(pieces, where), SHIFTS)]
    tile_cov = assigned_second(tiles, chunks, security_spans, *band, band_columns, owned, where)
    return (unpack_rows(arrived), col_cov, tile_cov)


def solution(mesh):
    placed = (P("tiles", "rows"), P(None, "rows"), P("tiles", "rows"), P(), P("rows", None))
    return jax.shard_map(
        on_device,
        mesh=mesh,
        in_specs=placed,
        out_specs=(P("tiles", "rows"), P("rows", "tiles", None), P("rows", "tiles", None, None)),
        check_vma=False,
    )
```

```python
import jax
import jax.numpy as jnp
from jax import lax
from jax.experimental import pallas as pl
from jax.experimental.pallas import tpu as pltpu
from jax.sharding import PartitionSpec as P

DAYS = 1024
PANEL = 512
BAND = 1024
N_X, N_Z, N_C, N_Y = 4, 8, 2, 4
PLANE = N_X * N_Z * N_C
LOCAL = DAYS // PLANE
QUARTER = BAND // N_Y
SLOTS = 2
SHARE = SLOTS * PANEL
WIDTH = 256
MAIN = SHARE + PANEL
FORCED = (1, 7, 2, 6, 3, 5)
PLANE_X = N_X * N_C
SHIFTS = [(0, 0), (1, 0), (3, 0), (2, 0), (0, 1), (1, 1), (3, 1), (2, 1)]
VMEM_LIMIT = 56 * 1024 * 1024


def params(limit=VMEM_LIMIT):
    return pltpu.CompilerParams(vmem_limit_bytes=limit)


def shape(*sizes, dtype=jnp.bfloat16):
    return jax.ShapeDtypeStruct(sizes, dtype)


def whole(*sizes):
    return pl.BlockSpec(sizes, lambda i, *_: (0,) * len(sizes))


def pack(returns, order, where):
    def body(order_ref, where_ref, in_ref, main_ref, *out_refs):
        def panel(owner, slot):
            start = pl.multiple_of(order_ref[owner * SLOTS + slot] * PANEL, PANEL)
            return in_ref[:, pl.ds(start, PANEL)]

        for k in range(N_Z):
            z = lax.rem(where_ref[1] + k, N_Z)
            for x in range(N_X):
                for core in range(N_C):
                    owner = (x * N_Z + z) * N_C + core
                    place = x * N_C + core
                    out_refs[k][:, place * PANEL : (place + 1) * PANEL] = panel(owner, 1)
        for owner in range(PLANE):
            main_ref[owner, :, :SHARE] = in_ref[:, owner * SHARE : (owner + 1) * SHARE]
            main_ref[owner, :, SHARE:] = panel(owner, 0)

    return pl.pallas_call(
        body,
        grid_spec=pltpu.PrefetchScalarGridSpec(
            num_scalar_prefetch=2,
            grid=(1,),
            in_specs=[whole(*returns.shape)],
            out_specs=[whole(PLANE, LOCAL, MAIN)] + [whole(LOCAL, PLANE_X * PANEL)] * N_Z,
        ),
        out_shape=[shape(PLANE, LOCAL, MAIN)] + [shape(LOCAL, PLANE_X * PANEL)] * N_Z,
        compiler_params=params(),
        name="pack",
    )(order, where, returns)


def repack(pieces, where):
    def body(where_ref, *refs):
        x, z, core = where_ref[0], where_ref[1], where_ref[2]
        for k in range(N_Z):
            rows = pl.ds(pl.multiple_of(lax.rem(z - k + N_Z, N_Z) * LOCAL, LOCAL), LOCAL)
            for j, (dx, dc) in enumerate(SHIFTS):
                target = lax.rem(x + dx, N_X) * N_C + lax.rem(core + dc, N_C)
                start = pl.multiple_of(target * PANEL, PANEL)
                refs[N_Z + j][rows, :] = refs[k][:, pl.ds(start, PANEL)]

    return pl.pallas_call(
        body,
        grid_spec=pltpu.PrefetchScalarGridSpec(
            num_scalar_prefetch=1,
            grid=(1,),
            in_specs=[whole(LOCAL, PLANE_X * PANEL)] * N_Z,
            out_specs=[whole(N_Z * LOCAL, PANEL)] * len(SHIFTS),
        ),
        out_shape=[shape(N_Z * LOCAL, PANEL)] * len(SHIFTS),
        compiler_params=params(),
        cost_estimate=pl.CostEstimate(flops=1 << 37, bytes_accessed=1 << 30, transcendentals=0),
        name="repack",
    )(where, *pieces)


def prepare_band(own, swapped, band_columns, where):
    def body(where_ref, spans_ref, own_ref, swapped_ref, masked_ref, mask_ref, days):
        k = pl.program_id(0)
        x, z, core, y = where_ref[0], where_ref[1], where_ref[2], where_ref[3]
        for side, part_ref in ((0, own_ref), (1, swapped_ref)):
            for j in range(N_X):
                for m in range(N_Z):
                    source = lax.rem(x - j + N_X, N_X) * N_Z + lax.rem(z - m // 2 - 4 * (m % 2) + N_Z, N_Z)
                    source = source * N_C + lax.rem(core + side, N_C)
                    days[pl.ds(pl.multiple_of(source * LOCAL, LOCAL), LOCAL), :] = part_ref[0, j, m * LOCAL : (m + 1) * LOCAL]
        rows = pl.ds(pl.multiple_of(lax.rem(y - k + N_Y, N_Y) * QUARTER, QUARTER), QUARTER)
        day = lax.broadcasted_iota(jnp.int32, (QUARTER, DAYS), 1)
        inside = (day >= spans_ref[rows, 0:1]) & (day <= spans_ref[rows, 1:2])
        flipped = jnp.transpose(days[...].astype(jnp.float32))
        masked_ref[rows, :] = jnp.where(inside, flipped, 0.0).astype(jnp.bfloat16)
        mask_ref[rows, :] = jnp.where(inside, 1.0, 0.0).astype(jnp.bfloat16)

    part = pl.BlockSpec((1, N_X, N_Z * LOCAL, QUARTER), lambda i, where: (i, 0, 0, 0))
    return pl.pallas_call(
        body,
        grid_spec=pltpu.PrefetchScalarGridSpec(
            num_scalar_prefetch=1,
            grid=(N_Y,),
            in_specs=[whole(BAND, 2), part, part],
            out_specs=[whole(BAND, DAYS)] * 2,
            scratch_shapes=[pltpu.VMEM((DAYS, QUARTER), jnp.bfloat16)],
        ),
        out_shape=[shape(BAND, DAYS)] * 2,
        compiler_params=params(),
        name="prepare_band",
    )(where, band_columns, own, swapped)


def listed(spans):
    day = lax.broadcasted_iota(jnp.int32, (DAYS, WIDTH), 0)
    return (day >= spans[0:1, :]) & (day <= spans[1:2, :])


def masked_returns(inside, column_returns):
    return jnp.where(inside, column_returns.astype(jnp.float32), 0.0).astype(jnp.bfloat16)


def scales(spans, band_columns):
    common = jnp.minimum(band_columns[:, 1:2], spans[1:2, :]) - jnp.maximum(band_columns[:, 0:1], spans[0:1, :]) + 1
    correlation = jnp.maximum(common, 0).astype(jnp.float32)
    return jnp.maximum(correlation, 1.0), 1.0 / jnp.maximum(correlation - 1.0, 1.0)


def factors(inside, spans, band_masked, band_columns):
    mask = jnp.where(inside, 1.0, 0.0).astype(jnp.bfloat16)
    band_sum = jnp.dot(band_masked, mask, preferred_element_type=jnp.float32)
    at_least, scale = scales(spans, band_columns)
    return scale, band_sum * scale / at_least


def covariance(spans, band_columns, band_masked, band_mask, column_returns):
    inside = listed(spans)
    masked = masked_returns(inside, column_returns)
    scale, mean = factors(inside, spans, band_masked, band_columns)
    gram = jnp.dot(band_masked, masked, preferred_element_type=jnp.float32)
    column_sum = jnp.dot(band_mask, masked, preferred_element_type=jnp.float32)
    return (gram * scale - column_sum * mean).astype(jnp.bfloat16)


def natural_means(spans, band_masked, band_columns, where):
    steps = SHARE // WIDTH

    def body(where_ref, spans_ref, band_ref, masked_ref, mean_ref):
        spans = spans_ref[...]
        _, mean_ref[...] = factors(listed(spans), spans, masked_ref[...], band_ref[...])

    return pl.pallas_call(
        body,
        grid_spec=pltpu.PrefetchScalarGridSpec(
            num_scalar_prefetch=1,
            grid=(steps,),
            in_specs=[
                pl.BlockSpec((2, WIDTH), lambda i, where: (0, where[4] * steps + i)),
                whole(BAND, 2),
                whole(BAND, DAYS),
            ],
            out_specs=pl.BlockSpec((BAND, WIDTH), lambda i, where: (0, i)),
        ),
        out_shape=shape(BAND, SHARE, dtype=jnp.float32),
        compiler_params=params(),
        name="natural_means",
    )(where, spans, band_columns, band_masked)


def natural_rows(fetched, spans, band_masked, band_mask, band_columns, mean, where):
    steps = SHARE // WIDTH

    def body(where_ref, spans_ref, band_ref, masked_ref, mask_ref, mean_ref, in_ref, rows_ref):
        spans = spans_ref[...]
        masked = masked_returns(listed(spans), in_ref[...])
        gram = jnp.dot(masked_ref[...], masked, preferred_element_type=jnp.float32)
        column_sum = jnp.dot(mask_ref[...], masked, preferred_element_type=jnp.float32)
        rows_ref[...] = (gram * scales(spans, band_ref[...])[1] - column_sum * mean_ref[...]).astype(jnp.bfloat16)

    return pl.pallas_call(
        body,
        grid_spec=pltpu.PrefetchScalarGridSpec(
            num_scalar_prefetch=1,
            grid=(steps,),
            in_specs=[
                pl.BlockSpec((2, WIDTH), lambda i, where: (0, where[4] * steps + i)),
                whole(BAND, 2),
                whole(BAND, DAYS),
                whole(BAND, DAYS),
                pl.BlockSpec((BAND, WIDTH), lambda i, where: (0, i)),
                pl.BlockSpec((DAYS, WIDTH), lambda i, where: (0, i)),
            ],
            out_specs=pl.BlockSpec((BAND, WIDTH), lambda i, where: (0, i)),
        ),
        out_shape=shape(BAND, SHARE),
        compiler_params=params(),
        cost_estimate=pl.CostEstimate(flops=6 * BAND * DAYS * SHARE, bytes_accessed=12 << 20, transcendentals=0),
        name="natural_rows",
    )(where, spans, band_columns, band_masked, band_mask, mean, fetched)


def flip(rows):
    def body(in_ref, out_ref):
        out_ref[0] = jnp.transpose(in_ref[...].astype(jnp.float32)).astype(jnp.bfloat16)

    return pl.pallas_call(
        body,
        grid=(SHARE // WIDTH,),
        in_specs=[pl.BlockSpec((BAND, WIDTH), lambda i: (0, i))],
        out_specs=pl.BlockSpec((1, WIDTH, BAND), lambda i: (0, i, 0)),
        out_shape=shape(1, SHARE, BAND),
        compiler_params=params(),
        name="flip",
    )(rows)


def assigned_first(fetched, spans, band_masked, band_mask, band_columns, owned):
    halves = PANEL // WIDTH

    def body(owned_ref, spans_ref, band_ref, masked_ref, mask_ref, in_ref, out_ref):
        out_ref[0, 0] = covariance(
            spans_ref[...], band_ref[...], masked_ref[...], mask_ref[...], in_ref[...]
        )

    return pl.pallas_call(
        body,
        grid_spec=pltpu.PrefetchScalarGridSpec(
            num_scalar_prefetch=1,
            grid=(halves,),
            in_specs=[
                pl.BlockSpec((2, WIDTH), lambda i, owned: (0, owned[0] * halves + i)),
                whole(BAND, 2),
                whole(BAND, DAYS),
                whole(BAND, DAYS),
                pl.BlockSpec((DAYS, WIDTH), lambda i, owned: (0, SHARE // WIDTH + i)),
            ],
            out_specs=pl.BlockSpec((1, 1, BAND, WIDTH), lambda i, owned: (0, 0, 0, i)),
        ),
        out_shape=shape(1, SLOTS, BAND, PANEL),
        compiler_params=params(),
        cost_estimate=pl.CostEstimate(flops=6 * BAND * DAYS * PANEL, bytes_accessed=6 << 20, transcendentals=0),
        name="assigned_first",
    )(owned, spans, band_columns, band_masked, band_mask, fetched)


def assigned_second(tiles, chunks, spans, band_masked, band_mask, band_columns, owned, where):
    halves = PANEL // WIDTH

    def body(owned_ref, where_ref, tiles_ref, spans_ref, band_ref, masked_ref, mask_ref, *refs):
        out_ref, days = refs[-2:]
        for j, (dx, dc) in enumerate(SHIFTS):
            x = lax.rem(where_ref[0] - dx + N_X, N_X)
            core = lax.rem(where_ref[2] + dc, N_C)
            for z in range(N_Z):
                start = pl.multiple_of(((x * N_Z + z) * N_C + core) * LOCAL, LOCAL)
                days[pl.ds(start, LOCAL), :] = refs[j][z * LOCAL : (z + 1) * LOCAL, :]
        out_ref[0, 0] = covariance(
            spans_ref[...], band_ref[...], masked_ref[...], mask_ref[...], days[...]
        )

    return pl.pallas_call(
        body,
        grid_spec=pltpu.PrefetchScalarGridSpec(
            num_scalar_prefetch=2,
            grid=(halves,),
            in_specs=[
                pl.BlockSpec(memory_space=pl.ANY),
                pl.BlockSpec((2, WIDTH), lambda i, owned, where: (0, owned[1] * halves + i)),
                whole(BAND, 2),
                whole(BAND, DAYS),
                whole(BAND, DAYS),
            ]
            + [pl.BlockSpec((N_Z * LOCAL, WIDTH), lambda i, owned, where: (0, i))] * len(SHIFTS),
            out_specs=pl.BlockSpec((1, 1, BAND, WIDTH), lambda i, owned, where: (0, 1, 0, i)),
            scratch_shapes=[pltpu.VMEM((DAYS, WIDTH), jnp.bfloat16)],
        ),
        out_shape=shape(1, SLOTS, BAND, PANEL),
        input_output_aliases={2: 0},
        compiler_params=params(),
        cost_estimate=pl.CostEstimate(flops=6 * BAND * DAYS * PANEL, bytes_accessed=6 << 20, transcendentals=0),
        name="assigned_second",
    )(owned, where, tiles, spans, band_columns, band_masked, band_mask, *chunks)


def unpack_rows(arrived):
    per_step = 32

    def body(in_ref, out_ref):
        for piece in range(per_step):
            out_ref[:, piece * SHARE : (piece + 1) * SHARE] = in_ref[piece]

    return pl.pallas_call(
        body,
        grid=(PLANE // per_step,),
        in_specs=[pl.BlockSpec((per_step, LOCAL, SHARE), lambda i: (i, 0, 0))],
        out_specs=pl.BlockSpec((LOCAL, per_step * SHARE), lambda i: (0, i)),
        out_shape=shape(LOCAL, PLANE * SHARE),
        compiler_params=params(24 * 1024 * 1024),
        name="unpack_rows",
    )(arrived)


def exchange(pieces):
    return lax.all_to_all(pieces, "tiles", split_axis=0, concat_axis=0, tiled=True)


def shift_rows(array, step):
    return lax.ppermute(array, "rows", [(y, (y + step) % N_Y) for y in range(N_Y)])


def swap(array, bit):
    return lax.ppermute(array, "tiles", [(i, i ^ bit) for i in range(PLANE)])


def shift(array, dx, dz, dc):
    def to(i):
        x, z, core = i // (N_Z * N_C) + dx, i // N_C % N_Z + dz, i % N_C + dc
        return (x % N_X * N_Z + z % N_Z) * N_C + core % N_C

    return lax.ppermute(array, "tiles", [(i, to(i)) for i in range(PLANE)])


def on_device(returns, security_spans, band_returns, band_spans, assignment):
    tile_index = lax.axis_index("tiles")
    x, z, core = tile_index // (N_Z * N_C), (tile_index // N_C) % N_Z, tile_index % N_C
    where = jnp.stack([x, z, core, lax.axis_index("rows"), tile_index]).astype(jnp.int32)
    order = assignment[0]
    owned = lax.dynamic_slice_in_dim(order, tile_index * SLOTS, SLOTS)
    band_columns = jnp.transpose(band_spans)

    packed, *sends = pack(returns, order, where)
    pair = jnp.concatenate([band_returns, shift(band_returns, 0, 4, 0)])
    pair, packed, sends = lax.optimization_barrier((pair, packed, sends))
    share = jnp.concatenate([pair] + [shift(pair, 0, k, 0) for k in range(1, 4)])
    packed, share = lax.optimization_barrier((packed, share))
    fetched = exchange(packed).reshape(DAYS, MAIN)
    own = jnp.stack([share] + [shift(share, j, 0, 0) for j in range(1, N_X)])
    own = jnp.stack([own] + [shift_rows(own, k) for k in range(1, N_Y)])
    swapped = swap(own, 1)
    band = prepare_band(own, swapped, band_columns, where)
    *band, sends = lax.optimization_barrier((*band, sends))
    pieces = [sends[0]] + [shift(sends[k], 0, k, 0) for k in range(1, N_Z)]

    mean = natural_means(security_spans, band[0], band_columns, where)
    rows = natural_rows(fetched, security_spans, *band, band_columns, mean, where)
    rows, fetched, *forced = lax.optimization_barrier((rows, fetched, *(pieces[k] for k in FORCED)))
    for k, piece in zip(FORCED, forced):
        pieces[k] = piece
    arrived = exchange(rows.reshape(PLANE, BAND // PLANE, SHARE))
    col_cov = flip(rows)
    tiles = assigned_first(fetched, security_spans, *band, band_columns, owned)
    chunks = [shift(part, dx, 0, dc) if dx or dc else part for part, (dx, dc) in zip(repack(pieces, where), SHIFTS)]
    tile_cov = assigned_second(tiles, chunks, security_spans, *band, band_columns, owned, where)
    return (unpack_rows(arrived), col_cov, tile_cov)


def solution(mesh):
    placed = (P("tiles", "rows"), P(None, "rows"), P("tiles", "rows"), P(), P("rows", None))
    return jax.shard_map(
        on_device,
        mesh=mesh,
        in_specs=placed,
        out_specs=(P("tiles", "rows"), P("rows", "tiles", None), P("rows", "tiles", None, None)),
        check_vma=False,
    )
```

```python
import jax
import jax.numpy as jnp
from jax import lax
from jax.experimental import pallas as pl
from jax.experimental.pallas import tpu as pltpu
from jax.sharding import PartitionSpec as P

DAYS = 1024
PANEL = 512
BAND = 1024
N_X, N_Z, N_C, N_Y = 4, 8, 2, 4
PLANE = N_X * N_Z * N_C
LOCAL = DAYS // PLANE
QUARTER = BAND // N_Y
SLOTS = 2
SHARE = SLOTS * PANEL
WIDTH = 256
MAIN = SHARE + PANEL
FORCED = (1, 7, 2, 6)
PLANE_X = N_X * N_C
SHIFTS = [(0, 0), (1, 0), (3, 0), (2, 0), (0, 1), (1, 1), (3, 1), (2, 1)]
VMEM_LIMIT = 56 * 1024 * 1024


def params(limit=VMEM_LIMIT):
    return pltpu.CompilerParams(vmem_limit_bytes=limit)


def shape(*sizes, dtype=jnp.bfloat16):
    return jax.ShapeDtypeStruct(sizes, dtype)


def whole(*sizes):
    return pl.BlockSpec(sizes, lambda i, *_: (0,) * len(sizes))


def pack(returns, order, where):
    def body(order_ref, where_ref, in_ref, main_ref, *out_refs):
        def panel(owner, slot):
            start = pl.multiple_of(order_ref[owner * SLOTS + slot] * PANEL, PANEL)
            return in_ref[:, pl.ds(start, PANEL)]

        for k in range(N_Z):
            z = lax.rem(where_ref[1] + k, N_Z)
            for x in range(N_X):
                for core in range(N_C):
                    owner = (x * N_Z + z) * N_C + core
                    place = x * N_C + core
                    out_refs[k][:, place * PANEL : (place + 1) * PANEL] = panel(owner, 1)
        for owner in range(PLANE):
            main_ref[owner, :, :SHARE] = in_ref[:, owner * SHARE : (owner + 1) * SHARE]
            main_ref[owner, :, SHARE:] = panel(owner, 0)

    return pl.pallas_call(
        body,
        grid_spec=pltpu.PrefetchScalarGridSpec(
            num_scalar_prefetch=2,
            grid=(1,),
            in_specs=[whole(*returns.shape)],
            out_specs=[whole(PLANE, LOCAL, MAIN)] + [whole(LOCAL, PLANE_X * PANEL)] * N_Z,
        ),
        out_shape=[shape(PLANE, LOCAL, MAIN)] + [shape(LOCAL, PLANE_X * PANEL)] * N_Z,
        compiler_params=params(),
        name="pack",
    )(order, where, returns)


def repack(pieces, where):
    def body(where_ref, *refs):
        x, z, core = where_ref[0], where_ref[1], where_ref[2]
        for k in range(N_Z):
            rows = pl.ds(pl.multiple_of(lax.rem(z - k + N_Z, N_Z) * LOCAL, LOCAL), LOCAL)
            for j, (dx, dc) in enumerate(SHIFTS):
                target = lax.rem(x + dx, N_X) * N_C + lax.rem(core + dc, N_C)
                start = pl.multiple_of(target * PANEL, PANEL)
                refs[N_Z + j][rows, :] = refs[k][:, pl.ds(start, PANEL)]

    return pl.pallas_call(
        body,
        grid_spec=pltpu.PrefetchScalarGridSpec(
            num_scalar_prefetch=1,
            grid=(1,),
            in_specs=[whole(LOCAL, PLANE_X * PANEL)] * N_Z,
            out_specs=[whole(N_Z * LOCAL, PANEL)] * len(SHIFTS),
        ),
        out_shape=[shape(N_Z * LOCAL, PANEL)] * len(SHIFTS),
        compiler_params=params(),
        cost_estimate=pl.CostEstimate(flops=1 << 37, bytes_accessed=1 << 30, transcendentals=0),
        name="repack",
    )(where, *pieces)


def prepare_band(own, swapped, band_columns, where):
    def body(where_ref, spans_ref, own_ref, swapped_ref, masked_ref, mask_ref, days):
        k = pl.program_id(0)
        x, z, core, y = where_ref[0], where_ref[1], where_ref[2], where_ref[3]
        for side, part_ref in ((0, own_ref), (1, swapped_ref)):
            for j in range(N_X):
                for m in range(N_Z):
                    source = lax.rem(x - j + N_X, N_X) * N_Z + lax.rem(z - m // 2 - 4 * (m % 2) + N_Z, N_Z)
                    source = source * N_C + lax.rem(core + side, N_C)
                    days[pl.ds(pl.multiple_of(source * LOCAL, LOCAL), LOCAL), :] = part_ref[0, j, m * LOCAL : (m + 1) * LOCAL]
        rows = pl.ds(pl.multiple_of(lax.rem(y - k + N_Y, N_Y) * QUARTER, QUARTER), QUARTER)
        day = lax.broadcasted_iota(jnp.int32, (QUARTER, DAYS), 1)
        inside = (day >= spans_ref[rows, 0:1]) & (day <= spans_ref[rows, 1:2])
        flipped = jnp.transpose(days[...].astype(jnp.float32))
        masked_ref[rows, :] = jnp.where(inside, flipped, 0.0).astype(jnp.bfloat16)
        mask_ref[rows, :] = jnp.where(inside, 1.0, 0.0).astype(jnp.bfloat16)

    part = pl.BlockSpec((1, N_X, N_Z * LOCAL, QUARTER), lambda i, where: (i, 0, 0, 0))
    return pl.pallas_call(
        body,
        grid_spec=pltpu.PrefetchScalarGridSpec(
            num_scalar_prefetch=1,
            grid=(N_Y,),
            in_specs=[whole(BAND, 2), part, part],
            out_specs=[whole(BAND, DAYS)] * 2,
            scratch_shapes=[pltpu.VMEM((DAYS, QUARTER), jnp.bfloat16)],
        ),
        out_shape=[shape(BAND, DAYS)] * 2,
        compiler_params=params(),
        name="prepare_band",
    )(where, band_columns, own, swapped)


def listed(spans):
    day = lax.broadcasted_iota(jnp.int32, (DAYS, WIDTH), 0)
    return (day >= spans[0:1, :]) & (day <= spans[1:2, :])


def masked_returns(inside, column_returns):
    return jnp.where(inside, column_returns.astype(jnp.float32), 0.0).astype(jnp.bfloat16)


def scales(spans, band_columns):
    common = jnp.minimum(band_columns[:, 1:2], spans[1:2, :]) - jnp.maximum(band_columns[:, 0:1], spans[0:1, :]) + 1
    correlation = jnp.maximum(common, 0).astype(jnp.float32)
    return jnp.maximum(correlation, 1.0), 1.0 / jnp.maximum(correlation - 1.0, 1.0)


def factors(inside, spans, band_masked, band_columns):
    mask = jnp.where(inside, 1.0, 0.0).astype(jnp.bfloat16)
    band_sum = jnp.dot(band_masked, mask, preferred_element_type=jnp.float32)
    at_least, scale = scales(spans, band_columns)
    return scale, band_sum * scale / at_least


def covariance(spans, band_columns, band_masked, band_mask, column_returns):
    inside = listed(spans)
    masked = masked_returns(inside, column_returns)
    scale, mean = factors(inside, spans, band_masked, band_columns)
    gram = jnp.dot(band_masked, masked, preferred_element_type=jnp.float32)
    column_sum = jnp.dot(band_mask, masked, preferred_element_type=jnp.float32)
    return (gram * scale - column_sum * mean).astype(jnp.bfloat16)


def natural_means(spans, band_masked, band_columns, where):
    steps = SHARE // WIDTH

    def body(where_ref, spans_ref, band_ref, masked_ref, mean_ref):
        spans = spans_ref[...]
        _, mean_ref[...] = factors(listed(spans), spans, masked_ref[...], band_ref[...])

    return pl.pallas_call(
        body,
        grid_spec=pltpu.PrefetchScalarGridSpec(
            num_scalar_prefetch=1,
            grid=(steps,),
            in_specs=[
                pl.BlockSpec((2, WIDTH), lambda i, where: (0, where[4] * steps + i)),
                whole(BAND, 2),
                whole(BAND, DAYS),
            ],
            out_specs=pl.BlockSpec((BAND, WIDTH), lambda i, where: (0, i)),
        ),
        out_shape=shape(BAND, SHARE, dtype=jnp.float32),
        compiler_params=params(),
        name="natural_means",
    )(where, spans, band_columns, band_masked)


def natural_rows(fetched, spans, band_masked, band_mask, band_columns, mean, where):
    steps = SHARE // WIDTH

    def body(where_ref, spans_ref, band_ref, masked_ref, mask_ref, mean_ref, in_ref, rows_ref):
        spans = spans_ref[...]
        masked = masked_returns(listed(spans), in_ref[...])
        gram = jnp.dot(masked_ref[...], masked, preferred_element_type=jnp.float32)
        column_sum = jnp.dot(mask_ref[...], masked, preferred_element_type=jnp.float32)
        rows_ref[...] = (gram * scales(spans, band_ref[...])[1] - column_sum * mean_ref[...]).astype(jnp.bfloat16)

    return pl.pallas_call(
        body,
        grid_spec=pltpu.PrefetchScalarGridSpec(
            num_scalar_prefetch=1,
            grid=(steps,),
            in_specs=[
                pl.BlockSpec((2, WIDTH), lambda i, where: (0, where[4] * steps + i)),
                whole(BAND, 2),
                whole(BAND, DAYS),
                whole(BAND, DAYS),
                pl.BlockSpec((BAND, WIDTH), lambda i, where: (0, i)),
                pl.BlockSpec((DAYS, WIDTH), lambda i, where: (0, i)),
            ],
            out_specs=pl.BlockSpec((BAND, WIDTH), lambda i, where: (0, i)),
        ),
        out_shape=shape(BAND, SHARE),
        compiler_params=params(),
        cost_estimate=pl.CostEstimate(flops=6 * BAND * DAYS * SHARE, bytes_accessed=12 << 20, transcendentals=0),
        name="natural_rows",
    )(where, spans, band_columns, band_masked, band_mask, mean, fetched)


def flip(rows):
    def body(in_ref, out_ref):
        out_ref[0] = jnp.transpose(in_ref[...].astype(jnp.float32)).astype(jnp.bfloat16)

    return pl.pallas_call(
        body,
        grid=(SHARE // WIDTH,),
        in_specs=[pl.BlockSpec((BAND, WIDTH), lambda i: (0, i))],
        out_specs=pl.BlockSpec((1, WIDTH, BAND), lambda i: (0, i, 0)),
        out_shape=shape(1, SHARE, BAND),
        compiler_params=params(),
        name="flip",
    )(rows)


def assigned_first(fetched, spans, band_masked, band_mask, band_columns, owned):
    halves = PANEL // WIDTH

    def body(owned_ref, spans_ref, band_ref, masked_ref, mask_ref, in_ref, out_ref):
        out_ref[0, 0] = covariance(
            spans_ref[...], band_ref[...], masked_ref[...], mask_ref[...], in_ref[...]
        )

    return pl.pallas_call(
        body,
        grid_spec=pltpu.PrefetchScalarGridSpec(
            num_scalar_prefetch=1,
            grid=(halves,),
            in_specs=[
                pl.BlockSpec((2, WIDTH), lambda i, owned: (0, owned[0] * halves + i)),
                whole(BAND, 2),
                whole(BAND, DAYS),
                whole(BAND, DAYS),
                pl.BlockSpec((DAYS, WIDTH), lambda i, owned: (0, SHARE // WIDTH + i)),
            ],
            out_specs=pl.BlockSpec((1, 1, BAND, WIDTH), lambda i, owned: (0, 0, 0, i)),
        ),
        out_shape=shape(1, SLOTS, BAND, PANEL),
        compiler_params=params(),
        cost_estimate=pl.CostEstimate(flops=6 * BAND * DAYS * PANEL, bytes_accessed=6 << 20, transcendentals=0),
        name="assigned_first",
    )(owned, spans, band_columns, band_masked, band_mask, fetched)


def assigned_second(tiles, chunks, spans, band_masked, band_mask, band_columns, owned, where):
    halves = PANEL // WIDTH

    def body(owned_ref, where_ref, tiles_ref, spans_ref, band_ref, masked_ref, mask_ref, *refs):
        out_ref, days = refs[-2:]
        for j, (dx, dc) in enumerate(SHIFTS):
            x = lax.rem(where_ref[0] - dx + N_X, N_X)
            core = lax.rem(where_ref[2] + dc, N_C)
            for z in range(N_Z):
                start = pl.multiple_of(((x * N_Z + z) * N_C + core) * LOCAL, LOCAL)
                days[pl.ds(start, LOCAL), :] = refs[j][z * LOCAL : (z + 1) * LOCAL, :]
        out_ref[0, 0] = covariance(
            spans_ref[...], band_ref[...], masked_ref[...], mask_ref[...], days[...]
        )

    return pl.pallas_call(
        body,
        grid_spec=pltpu.PrefetchScalarGridSpec(
            num_scalar_prefetch=2,
            grid=(halves,),
            in_specs=[
                pl.BlockSpec(memory_space=pl.ANY),
                pl.BlockSpec((2, WIDTH), lambda i, owned, where: (0, owned[1] * halves + i)),
                whole(BAND, 2),
                whole(BAND, DAYS),
                whole(BAND, DAYS),
            ]
            + [pl.BlockSpec((N_Z * LOCAL, WIDTH), lambda i, owned, where: (0, i))] * len(SHIFTS),
            out_specs=pl.BlockSpec((1, 1, BAND, WIDTH), lambda i, owned, where: (0, 1, 0, i)),
            scratch_shapes=[pltpu.VMEM((DAYS, WIDTH), jnp.bfloat16)],
        ),
        out_shape=shape(1, SLOTS, BAND, PANEL),
        input_output_aliases={2: 0},
        compiler_params=params(),
        cost_estimate=pl.CostEstimate(flops=6 * BAND * DAYS * PANEL, bytes_accessed=6 << 20, transcendentals=0),
        name="assigned_second",
    )(owned, where, tiles, spans, band_columns, band_masked, band_mask, *chunks)


def unpack_rows(arrived):
    def body(in_ref, out_ref, done):
        copies = [
            pltpu.make_async_copy(in_ref.at[piece], out_ref.at[:, pl.ds(piece * SHARE, SHARE)], done.at[piece])
            for piece in range(PLANE)
        ]
        for copy in copies:
            copy.start()
        for copy in copies:
            copy.wait()

    return pl.pallas_call(
        body,
        in_specs=[pl.BlockSpec(memory_space=pl.ANY)],
        out_specs=pl.BlockSpec(memory_space=pl.ANY),
        out_shape=shape(LOCAL, PLANE * SHARE),
        scratch_shapes=[pltpu.SemaphoreType.DMA((PLANE,))],
        compiler_params=params(24 * 1024 * 1024),
        name="unpack_rows",
    )(arrived)


def exchange(pieces):
    return lax.all_to_all(pieces, "tiles", split_axis=0, concat_axis=0, tiled=True)


def shift_rows(array, step):
    return lax.ppermute(array, "rows", [(y, (y + step) % N_Y) for y in range(N_Y)])


def swap(array, bit):
    return lax.ppermute(array, "tiles", [(i, i ^ bit) for i in range(PLANE)])


def shift(array, dx, dz, dc):
    def to(i):
        x, z, core = i // (N_Z * N_C) + dx, i // N_C % N_Z + dz, i % N_C + dc
        return (x % N_X * N_Z + z % N_Z) * N_C + core % N_C

    return lax.ppermute(array, "tiles", [(i, to(i)) for i in range(PLANE)])


def on_device(returns, security_spans, band_returns, band_spans, assignment):
    tile_index = lax.axis_index("tiles")
    x, z, core = tile_index // (N_Z * N_C), (tile_index // N_C) % N_Z, tile_index % N_C
    where = jnp.stack([x, z, core, lax.axis_index("rows"), tile_index]).astype(jnp.int32)
    order = assignment[0]
    owned = lax.dynamic_slice_in_dim(order, tile_index * SLOTS, SLOTS)
    band_columns = jnp.transpose(band_spans)

    packed, *sends = pack(returns, order, where)
    pair = jnp.concatenate([band_returns, shift(band_returns, 0, 4, 0)])
    pair, packed, sends = lax.optimization_barrier((pair, packed, sends))
    share = jnp.concatenate([pair] + [shift(pair, 0, k, 0) for k in range(1, 4)])
    packed, share = lax.optimization_barrier((packed, share))
    fetched = exchange(packed).reshape(DAYS, MAIN)
    own = jnp.stack([share] + [shift(share, j, 0, 0) for j in range(1, N_X)])
    own = jnp.stack([own] + [shift_rows(own, k) for k in range(1, N_Y)])
    swapped = swap(own, 1)
    band = prepare_band(own, swapped, band_columns, where)
    *band, sends = lax.optimization_barrier((*band, sends))
    pieces = [sends[0]] + [shift(sends[k], 0, k, 0) for k in range(1, N_Z)]

    mean = natural_means(security_spans, band[0], band_columns, where)
    rows = natural_rows(fetched, security_spans, *band, band_columns, mean, where)
    rows, fetched, *forced = lax.optimization_barrier((rows, fetched, *(pieces[k] for k in FORCED)))
    for k, piece in zip(FORCED, forced):
        pieces[k] = piece
    arrived = exchange(rows.reshape(PLANE, BAND // PLANE, SHARE))
    col_cov = flip(rows)
    tiles = assigned_first(fetched, security_spans, *band, band_columns, owned)
    chunks = [shift(part, dx, 0, dc) if dx or dc else part for part, (dx, dc) in zip(repack(pieces, where), SHIFTS)]
    tile_cov = assigned_second(tiles, chunks, security_spans, *band, band_columns, owned, where)
    return (unpack_rows(arrived), col_cov, tile_cov)


def solution(mesh):
    placed = (P("tiles", "rows"), P(None, "rows"), P("tiles", "rows"), P(), P("rows", None))
    return jax.shard_map(
        on_device,
        mesh=mesh,
        in_specs=placed,
        out_specs=(P("tiles", "rows"), P("rows", "tiles", None), P("rows", "tiles", None, None)),
        check_vma=False,
    )
```
